32 devices in a mesh: grp: 2 (over x), sp: 8 (over z, y), ch: 2 (over core).
Axes of the slice: x: 2, y: 2, z: 4, core: 2. Of those that a mesh axis runs over, the one named last changes fastest.
Arguments:
- grid_tokens: bfloat16 [16, 128, 2048], P(('grp', 'sp'), None, 'ch'), parts along dimension 0, may hold values from -6 to 6
- conv_weight: float32 [3, 3, 2048], P(None, None, 'ch'), may hold values from -2 to 2
- norm_gain: float32 [2048], replicated, may hold values from 0.1 to 1.9
- qkv_weight: bfloat16 [2048, 3, 2048], P('sp', None, 'ch'), may hold values from -1 to 1
Outputs:
- attended: bfloat16 [16, 128, 2048], P(('grp', 'sp'), None, 'ch'), parts along dimension 0
The draws below stay inside these ranges and needn't reach their ends.
There are 2 independent parts, one for each index of `grp`. The reference program is written for one: setup_inputs(seed, part) draws one part's arguments, and reference() takes and returns one part's arrays. A program takes and returns all parts, laid end to end along the dimension named above; an argument that names none is the same for every part. Nothing has to cross between parts.
All inputs are finite; a program needn't handle non-finite values.
Results may differ from the reference program's by a relative error of at most 0.0097.
Values may be sent and summed in bfloat16 or wider, within the bound.
A program may use at most 128 MiB of HBM per device.

```python
import jax
import jax.numpy as jnp
from jax import lax

D = 2048
HEAD_DIM = 64
GRID_W = 128
HEADS = 32
GRID_H = 8


def draw_qkv_weight(key, part):
    base = jax.random.normal(key, (D, 3, D), jnp.float32) * D ** (-0.5)
    return jnp.clip(base, -1.0, 1.0).astype(jnp.bfloat16)


def block_scale(rng, shape, cuts, least, top_value):
    loudness = 1.0
    for dim, blocks in cuts:
        draws = jax.random.uniform(jax.random.fold_in(jax.random.fold_in(rng, 6), dim), (blocks,), jnp.float32, least / len(cuts), top_value / len(cuts))
        loudness = loudness * jnp.repeat(jnp.exp(draws), shape[dim] // blocks).reshape((-1,) + (1,) * (len(shape) - 1 - dim))
    return loudness


def gaussian(rng, dims, scale, bound, pieces=(), dtype=jnp.bfloat16):
    array = scale * jax.random.normal(rng, dims, jnp.float32)
    if pieces:
        array = array * block_scale(rng, dims, pieces, -0.22, 0.18)
    return jnp.clip(array, -bound, bound).astype(dtype)


def setup_inputs(seed: int = 0, part: int = 0) -> dict:
    key_list = jax.random.split(jax.random.key(seed), 5)
    part_splits = jax.random.split(jax.random.fold_in(key_list[4], part), 5)
    grid_tokens = gaussian(part_splits[0], (GRID_H, GRID_W, D), 1.0, 6.0, ((0, 8), (2, 2)))
    conv_weight = gaussian(key_list[1], (3, 3, D), 9 ** -0.5, 2.0, ((2, 2),), jnp.float32)
    norm_gain = jnp.clip(1.0 + 0.18 * jax.random.normal(key_list[2], (D,), jnp.float32), 0.1, 1.9)
    qkv_weight = draw_qkv_weight(jax.random.fold_in(key_list[4], 71), part)
    return {"grid_tokens": grid_tokens, "conv_weight": conv_weight, "norm_gain": norm_gain, "qkv_weight": qkv_weight}


def reference(grid_tokens, conv_weight, norm_gain, qkv_weight):
    source = grid_tokens.astype(jnp.float32)
    padded = jnp.pad(source, ((1, 1), (1, 1), (0, 0)))
    rows, cols = (source.shape[0], source.shape[1])
    conv = jnp.zeros_like(source)
    for row_off in range(3):
        for col_off in range(3):
            conv = conv + padded[row_off:row_off + rows, col_off:col_off + cols] * conv_weight[row_off, col_off]
    mixed = (source + conv).astype(jnp.bfloat16)
    flat = mixed.astype(jnp.float32).reshape(rows * cols, D)
    mean = lax.optimization_barrier(jnp.mean(flat, axis=1, keepdims=True))
    var = lax.optimization_barrier(jnp.mean((flat - mean) ** 2, axis=1, keepdims=True))
    normed = ((flat - mean) / jnp.sqrt(var + 1e-06) * norm_gain).astype(jnp.bfloat16)
    proj = jnp.dot(normed, qkv_weight.reshape(D, 3 * D), preferred_element_type=jnp.float32).astype(jnp.bfloat16)
    count = rows * cols
    query = proj[:, :D].reshape(count, HEADS, HEAD_DIM).transpose(1, 0, 2)
    key = proj[:, D:2 * D].reshape(count, HEADS, HEAD_DIM).transpose(1, 0, 2)
    value = proj[:, 2 * D:].reshape(count, HEADS, HEAD_DIM).transpose(1, 0, 2)

    def one_head(items):
        q_head, k_head, v_head = items
        scores = jnp.dot(q_head, k_head.T, preferred_element_type=jnp.float32) / jnp.sqrt(jnp.float32(HEAD_DIM))
        top = lax.optimization_barrier(jnp.max(scores, axis=1, keepdims=True))
        expo = jnp.exp(scores - top)
        total = lax.optimization_barrier(jnp.sum(expo, axis=1, keepdims=True))
        probs = expo.astype(jnp.bfloat16)
        return jnp.dot(probs, v_head, preferred_element_type=jnp.float32) / total
    heads_out = lax.map(one_head, (query, key, value))
    attended = heads_out.transpose(1, 0, 2).reshape(rows, cols, D)
    return attended.astype(jnp.bfloat16)
```

```python
import functools

import jax
import jax.numpy as jnp
from jax import lax
from jax.experimental import pallas as pl
from jax.experimental.pallas import tpu as pltpu
from jax.sharding import PartitionSpec as P

D = 2048
HEAD_DIM = 64


def with_halo(block, sides, width):
    for axis, dim in sides:
        count = lax.axis_size(axis)
        forward = [(i, i + 1) for i in range(count - 1)]
        backward = [(target, source) for source, target in forward]
        low = lax.ppermute(
            lax.slice_in_dim(block, block.shape[dim] - width, None, axis=dim), axis, forward
        )
        high = lax.ppermute(lax.slice_in_dim(block, 0, width, axis=dim), axis, backward)
        block = jnp.concatenate([low, block, high], axis=dim)
    return block


def make_attend(query, heads_n):
    inv_scale = 1.0 / jnp.sqrt(jnp.float32(HEAD_DIM))

    def attend(carry, pieces, start):
        running_top, running_total, accum = carry
        key_piece, value_piece = pieces
        width = key_piece.shape[0]
        key_heads = key_piece.reshape(width, heads_n, HEAD_DIM)
        value_heads = value_piece.reshape(width, heads_n, HEAD_DIM)
        scores = (
            jnp.einsum("thd,nhd->htn", query, key_heads, preferred_element_type=jnp.float32)
            * inv_scale
        )
        new_top = jnp.maximum(running_top, jnp.max(scores, axis=2))
        expo = jnp.exp(scores - new_top[:, :, None])
        new_total = jnp.sum(expo, axis=2)
        probs = expo.astype(jnp.bfloat16)
        update = jnp.einsum("htn,nhd->htd", probs, value_heads, preferred_element_type=jnp.float32)
        return (new_top, new_total, update)

    return attend


def start_state(heads_n, queries_n):
    return (
        jnp.full((heads_n, queries_n), -1e30, jnp.float32),
        jnp.zeros((heads_n, queries_n), jnp.float32),
        jnp.zeros((heads_n, queries_n, HEAD_DIM), jnp.float32),
    )


def local_gathered(grid_tokens, conv_weight, norm_gain, qkv_weight):
    rows, cols, local_ch = grid_tokens.shape
    count = rows * cols
    heads_here = local_ch // HEAD_DIM
    extended = with_halo(grid_tokens, (("sp", 0),), 1)
    padded = jnp.pad(extended.astype(jnp.float32), ((0, 0), (1, 1), (0, 0)))
    conv = jnp.zeros((rows, cols, local_ch), jnp.float32)
    for row_off in range(3):
        for col_off in range(3):
            conv = (
                conv
                + padded[row_off : row_off + rows, col_off : col_off + cols]
                * conv_weight[row_off, col_off]
            )
    mixed = (grid_tokens.astype(jnp.float32) + conv).astype(jnp.bfloat16)
    full = lax.all_gather(mixed, "ch", axis=2, tiled=True)
    flat = full.astype(jnp.float32).reshape(count, D)
    mean = jnp.mean(flat, axis=1, keepdims=True)
    var = jnp.mean((flat - mean) ** 2, axis=1, keepdims=True)
    normed = ((flat - mean) * lax.rsqrt(var + 1e-06) * norm_gain).astype(jnp.bfloat16)
    panel = lax.all_gather(qkv_weight, "sp", axis=0, tiled=True)
    proj = jnp.dot(normed, panel.reshape(D, 3 * local_ch), preferred_element_type=jnp.float32)
    proj = proj.astype(jnp.bfloat16)
    query_local = proj[:, :local_ch]
    key_local = proj[:, local_ch : 2 * local_ch]
    value_local = proj[:, 2 * local_ch :]
    query = query_local.reshape(count, heads_here, HEAD_DIM)
    attend = make_attend(query, heads_here)
    init = start_state(heads_here, count)
    final = attend(
        init,
        (
            lax.all_gather(key_local, "sp", axis=0, tiled=True),
            lax.all_gather(value_local, "sp", axis=0, tiled=True),
        ),
        jnp.int32(0),
    )
    result = final[2] / final[1][:, :, None]
    result = result.transpose(1, 0, 2).reshape(rows, cols, local_ch)
    return result.astype(jnp.bfloat16)


MESH = pl.DeviceIdType.MESH


def fused_kernel(
    n, x_ref, conv_ref, gain_ref, w_ref, out_ref,
    halo, mix, xs, ws, qs, ks, vs, os,
    halo_send, halo_recv, own_sem, w_send, w_recv, f_send, f_recv, mix_send, mix_recv,
    ring_send, ring_recv, peer_send, peer_recv, out_send, out_recv,
):
    tokens, local_ch = x_ref.shape
    depth, wide = w_ref.shape[1], qs.shape[1]
    share, half = depth // 2, n // 2
    g, s, c = lax.axis_index("grp"), lax.axis_index("sp"), lax.axis_index("ch")
    pos = (s % 2) * (n - 1) + (1 - 2 * (s % 2)) * (s // 2)

    def at_ring(p):
        p = lax.rem(p + 2 * n, n)
        back = p // half
        return 2 * (p * (1 - back) + (n - 1 - p) * back) + back

    def send(src, dst, send_sem, recv_sem, to):
        return pltpu.make_async_remote_copy(
            src_ref=src, dst_ref=dst, send_sem=send_sem, recv_sem=recv_sem,
            device_id=to, device_id_type=MESH,
        )

    other_group, other_core = (1 - g, s, c), (g, s, 1 - c)

    barrier = pltpu.get_barrier_semaphore()
    for k in range(1, n):
        pl.semaphore_signal(barrier, inc=1, device_id=(g, lax.rem(s + k, n), c), device_id_type=MESH)
    pl.semaphore_signal(barrier, inc=1, device_id=other_group, device_id_type=MESH)
    pl.semaphore_signal(barrier, inc=1, device_id=other_core, device_id_type=MESH)
    pl.semaphore_wait(barrier, n + 1)

    def halo_down():
        return send(x_ref, halo.at[0], halo_send.at[0], halo_recv.at[0], (g, lax.rem(s + 1, n), c))

    def halo_up():
        return send(x_ref, halo.at[1], halo_send.at[1], halo_recv.at[1], (g, lax.rem(s + n - 1, n), c))

    @pl.when(s < n - 1)
    def _():
        halo_down().start()

    @pl.when(s > 0)
    def _():
        halo_up().start()

    def w_copy(k):
        to = lax.rem(s + k, n)
        cols = pl.ds(pl.multiple_of(to * wide, wide), wide)
        return send(
            w_ref.at[:, pl.ds(g * share, share), cols],
            ws.at[:, pl.ds(s * depth + g * share, share), :],
            w_send.at[k], w_recv.at[k], (g, to, c),
        )

    def w_arrived(k):
        origin = lax.rem(s + n - k, n)
        rows = ws.at[:, pl.ds(origin * depth + g * share, share), :]
        return send(rows, rows, f_send.at[k], w_recv.at[k], other_group)

    def w_forward(k):
        origin = lax.rem(s + n - k, n)
        rows = ws.at[:, pl.ds(origin * depth + g * share, share), :]
        return send(rows, rows, f_send.at[k], f_recv.at[k], other_group)

    def w_forward_in(k):
        origin = lax.rem(s + n - k, n)
        rows = ws.at[:, pl.ds(origin * depth + (1 - g) * share, share), :]
        return send(rows, rows, f_send.at[k], f_recv.at[k], other_group)

    own_w = pltpu.make_async_copy(
        w_ref.at[:, :, pl.ds(pl.multiple_of(s * wide, wide), wide)],
        ws.at[:, pl.ds(s * depth, depth), :],
        own_sem,
    )
    own_w.start()

    def start_w(k, _):
        w_copy(k).start()
        return 0

    lax.fori_loop(1, n, start_w, 0)

    @pl.when(s > 0)
    def _():
        halo_down().wait_recv()

    @pl.when(s == 0)
    def _():
        halo[0] = jnp.zeros((tokens, local_ch), jnp.bfloat16)

    @pl.when(s < n - 1)
    def _():
        halo_up().wait_recv()

    @pl.when(s == n - 1)
    def _():
        halo[1] = jnp.zeros((tokens, local_ch), jnp.bfloat16)

    def conv_part(i, _):
        cols = pl.ds(pl.multiple_of(i * 128, 128), 128)
        above = halo[0, :, cols].astype(jnp.float32)
        here = x_ref[:, cols].astype(jnp.float32)
        below = halo[1, :, cols].astype(jnp.float32)
        weight = conv_ref[:, :, cols]

        def column(b):
            return above * weight[0, b : b + 1] + here * weight[1, b : b + 1] + below * weight[2, b : b + 1]

        token = lax.broadcasted_iota(jnp.int32, (tokens, 128), 0)
        left = jnp.where(token == 0, 0.0, pltpu.roll(column(0), 1, 0))
        right = jnp.where(token == tokens - 1, 0.0, pltpu.roll(column(2), tokens - 1, 0))
        mix[c, :, cols] = (here + (left + column(1) + right)).astype(jnp.bfloat16)
        return 0

    lax.fori_loop(0, local_ch // 128, conv_part, 0)

    to_peer = send(mix.at[c], mix.at[c], mix_send, mix_recv, other_core)
    to_peer.start()
    send(mix.at[1 - c], mix.at[1 - c], mix_send, mix_recv, other_core).wait_recv()

    def norm_part(i, _):
        rows = pl.ds(pl.multiple_of(i * 16, 16), 16)
        first = mix[0, rows, :].astype(jnp.float32)
        second = mix[1, rows, :].astype(jnp.float32)
        channels = 2 * local_ch
        mean = (jnp.sum(first, axis=1, keepdims=True) + jnp.sum(second, axis=1, keepdims=True)) / channels
        first, second = first - mean, second - mean
        var = (
            jnp.sum(first * first, axis=1, keepdims=True) + jnp.sum(second * second, axis=1, keepdims=True)
        ) / channels
        scale = lax.rsqrt(var + 1e-06)
        xs[s, 0, rows, :] = (first * scale * gain_ref[:, :local_ch]).astype(jnp.bfloat16)
        xs[s, 1, rows, :] = (second * scale * gain_ref[:, local_ch:]).astype(jnp.bfloat16)
        return 0

    lax.fori_loop(0, tokens // 16, norm_part, 0)

    def ring_block(way, k):
        owner = at_ring(pos - k if way == 0 else pos + k)
        if k < half:
            return xs.at[owner, c]
        return xs.at[owner, c, pl.ds(way * (tokens // 2), tokens // 2)]

    def ring_copy(way, k):
        owner = at_ring(pos - (k - 1) if way == 0 else pos + (k - 1))
        part = xs.at[owner, c] if k < half else xs.at[owner, c, pl.ds(way * (tokens // 2), tokens // 2)]
        to = (g, at_ring(pos + 1 if way == 0 else pos - 1), c)
        return send(part, part, ring_send.at[way, k], ring_recv.at[way, k], to)

    def ring_arrived(way, k):
        part = ring_block(way, k)
        return send(part, part, ring_send.at[way, k], ring_recv.at[way, k], other_core)

    def peer_copy(way, k):
        part = ring_block(way, k)
        return send(part, part, peer_send.at[way, k], peer_recv.at[way, k], other_core)

    def peer_arrived(way, k):
        owner = at_ring(pos - k if way == 0 else pos + k)
        part = xs.at[owner, 1 - c]
        if k == half:
            part = xs.at[owner, 1 - c, pl.ds(way * (tokens // 2), tokens // 2)]
        return send(part, part, peer_send.at[way, k], peer_recv.at[way, k], other_core)

    def project(owner):
        total = []
        for lo, hi in ((0, 1), (1, 3)):
            value = jnp.zeros((tokens, (hi - lo) * wide), jnp.float32)
            for h in range(2):
                weight = jnp.concatenate([ws[j, h * local_ch : (h + 1) * local_ch] for j in range(lo, hi)], axis=1)
                value = value + jnp.dot(xs[owner, h], weight, preferred_element_type=jnp.float32)
            total.append(value)
        rows = pl.ds(pl.multiple_of(owner * tokens, tokens), tokens)
        qs[rows, :] = total[0].astype(jnp.bfloat16)
        ks[rows, :] = total[1][:, :wide].astype(jnp.bfloat16)
        vs[rows, :] = total[1][:, wide:].astype(jnp.bfloat16)

    def project_pair(k):
        def one(i, _):
            project(at_ring(pos - k + 2 * k * i))
            return 0

        lax.fori_loop(0, 2, one, 0)

    for way in range(2):
        ring_copy(way, 1).start()

    def forward_w(k, _):
        w_arrived(k).wait_recv()
        w_forward(k).start()
        return 0

    lax.fori_loop(1, n, forward_w, 0)

    for k in range(1, half + 1):
        for way in range(2):
            ring_arrived(way, k).wait_recv()
            if k < half:
                ring_copy(way, k + 1).start()
            peer_copy(way, k).start()
        if k == 1:
            own_w.wait()

            def w_last(j, _):
                w_forward_in(j).wait_recv()
                return 0

            lax.fori_loop(1, n, w_last, 0)
            project(s)
        else:
            for way in range(2):
                peer_arrived(way, k - 1).wait_recv()
            project_pair(k - 1)
    for way in range(2):
        peer_arrived(way, half).wait_recv()
    project(at_ring(pos + half))

    def out_copy(i):
        to = lax.rem(s + 1 + i, n)
        return send(
            os.at[i], out_ref.at[:, pl.ds(pl.multiple_of(s * wide, wide), wide)],
            out_send.at[i], out_recv.at[i], (g, to, c),
        )

    def out_arrived(i):
        origin = lax.rem(s + 2 * n - 1 - i, n)
        return send(
            os.at[i], out_ref.at[:, pl.ds(pl.multiple_of(origin * wide, wide), wide)],
            out_send.at[i], out_recv.at[i], other_core,
        )

    heads = wide // HEAD_DIM

    def attend_block(i, _):
        block = lax.rem(s + 1 + i, n)
        query = qs[pl.ds(pl.multiple_of(block * tokens, tokens), tokens), :]
        lane = lax.broadcasted_iota(jnp.int32, (tokens, wide), 1) // HEAD_DIM
        result = jnp.zeros((tokens, wide), jnp.float32)
        for h in range(heads):
            own = jnp.where(lane == h, query.astype(jnp.float32) * HEAD_DIM**-0.5, 0.0).astype(jnp.bfloat16)
            scores = lax.dot_general(
                own, ks[...], (((1,), (1,)), ((), ())), preferred_element_type=jnp.float32
            )
            top = jnp.max(scores, axis=1, keepdims=True)
            expo = jnp.exp(scores - top)
            total = jnp.sum(expo, axis=1, keepdims=True)
            part = jnp.dot(expo.astype(jnp.bfloat16), vs[...], preferred_element_type=jnp.float32)
            result = jnp.where(lane == h, part / total, result)
        os[i] = result.astype(jnp.bfloat16)

        @pl.when(i < n - 1)
        def _():
            out_copy(i).start()

        return 0

    lax.fori_loop(0, n, attend_block, 0)
    out_ref[:, pl.ds(pl.multiple_of(s * wide, wide), wide)] = os[n - 1]

    @pl.when(s < n - 1)
    def _():
        halo_down().wait_send()

    @pl.when(s > 0)
    def _():
        halo_up().wait_send()

    def sent_w(k, _):
        w_copy(k).wait_send()
        w_forward(k).wait_send()
        return 0

    lax.fori_loop(1, n, sent_w, 0)
    to_peer.wait_send()
    for k in range(1, half + 1):
        for way in range(2):
            ring_copy(way, k).wait_send()
            peer_copy(way, k).wait_send()

    def out_done(i, _):
        out_copy(i).wait_send()
        out_arrived(i).wait_recv()
        return 0

    lax.fori_loop(0, n - 1, out_done, 0)


def local_fused(n, grid_tokens, conv_weight, norm_gain, qkv_weight):
    rows, cols, local_ch = grid_tokens.shape
    depth = qkv_weight.shape[0]
    wide = local_ch // n
    count = n * cols
    dma = pltpu.SemaphoreType.DMA
    vmem = pl.BlockSpec(memory_space=pltpu.VMEM)
    half = n // 2
    out = pl.pallas_call(
        functools.partial(fused_kernel, n),
        out_shape=jax.ShapeDtypeStruct((cols, local_ch), jnp.bfloat16),
        in_specs=[vmem, vmem, vmem, pl.BlockSpec(memory_space=pl.ANY)],
        out_specs=vmem,
        scratch_shapes=[
            pltpu.VMEM((2, cols, local_ch), jnp.bfloat16),
            pltpu.VMEM((2, cols, local_ch), jnp.bfloat16),
            pltpu.VMEM((n, 2, cols, local_ch), jnp.bfloat16),
            pltpu.VMEM((3, n * depth, wide), jnp.bfloat16),
            pltpu.VMEM((count, wide), jnp.bfloat16),
            pltpu.VMEM((count, wide), jnp.bfloat16),
            pltpu.VMEM((count, wide), jnp.bfloat16),
            pltpu.VMEM((n, cols, wide), jnp.bfloat16),
            dma((2,)), dma((2,)), dma, dma((n,)), dma((n,)), dma((n,)), dma((n,)), dma, dma,
            dma((2, half + 1)), dma((2, half + 1)), dma((2, half + 1)), dma((2, half + 1)),
            dma((n,)), dma((n,)),
        ],
        compiler_params=pltpu.CompilerParams(
            collective_id=0, has_side_effects=True, vmem_limit_bytes=40 * 1024 * 1024
        ),
    )(
        grid_tokens.reshape(cols, local_ch), conv_weight, norm_gain.reshape(1, D),
        qkv_weight.transpose(1, 0, 2),
    )
    return out.reshape(rows, cols, local_ch)


def solution(mesh):
    placed = (P(("grp", "sp"), None, "ch"), P(None, None, "ch"), P(), P("sp", None, "ch"))
    groups, n, cores = mesh.shape["grp"], mesh.shape["sp"], mesh.shape["ch"]

    def local(grid_tokens, conv_weight, norm_gain, qkv_weight):
        rows, _, local_ch = grid_tokens.shape
        if groups == 2 and cores == 2 and n % 4 == 0 and rows == 1 and local_ch == 128 * n:
            return local_fused(n, grid_tokens, conv_weight, norm_gain, qkv_weight)
        return local_gathered(grid_tokens, conv_weight, norm_gain, qkv_weight)

    return jax.shard_map(
        local, mesh=mesh, in_specs=placed, out_specs=P(("grp", "sp"), None, "ch"), check_vma=False
    )
```

```python
import functools

import jax
import jax.numpy as jnp
from jax import lax
from jax.experimental import pallas as pl
from jax.experimental.pallas import tpu as pltpu
from jax.sharding import PartitionSpec as P

D = 2048
HEAD_DIM = 64


def with_halo(block, sides, width):
    for axis, dim in sides:
        count = lax.axis_size(axis)
        forward = [(i, i + 1) for i in range(count - 1)]
        backward = [(target, source) for source, target in forward]
        low = lax.ppermute(
            lax.slice_in_dim(block, block.shape[dim] - width, None, axis=dim), axis, forward
        )
        high = lax.ppermute(lax.slice_in_dim(block, 0, width, axis=dim), axis, backward)
        block = jnp.concatenate([low, block, high], axis=dim)
    return block


def make_attend(query, heads_n):
    inv_scale = 1.0 / jnp.sqrt(jnp.float32(HEAD_DIM))

    def attend(carry, pieces, start):
        running_top, running_total, accum = carry
        key_piece, value_piece = pieces
        width = key_piece.shape[0]
        key_heads = key_piece.reshape(width, heads_n, HEAD_DIM)
        value_heads = value_piece.reshape(width, heads_n, HEAD_DIM)
        scores = (
            jnp.einsum("thd,nhd->htn", query, key_heads, preferred_element_type=jnp.float32)
            * inv_scale
        )
        new_top = jnp.maximum(running_top, jnp.max(scores, axis=2))
        expo = jnp.exp(scores - new_top[:, :, None])
        new_total = jnp.sum(expo, axis=2)
        probs = expo.astype(jnp.bfloat16)
        update = jnp.einsum("htn,nhd->htd", probs, value_heads, preferred_element_type=jnp.float32)
        return (new_top, new_total, update)

    return attend


def start_state(heads_n, queries_n):
    return (
        jnp.full((heads_n, queries_n), -1e30, jnp.float32),
        jnp.zeros((heads_n, queries_n), jnp.float32),
        jnp.zeros((heads_n, queries_n, HEAD_DIM), jnp.float32),
    )


def local_gathered(grid_tokens, conv_weight, norm_gain, qkv_weight):
    rows, cols, local_ch = grid_tokens.shape
    count = rows * cols
    heads_here = local_ch // HEAD_DIM
    extended = with_halo(grid_tokens, (("sp", 0),), 1)
    padded = jnp.pad(extended.astype(jnp.float32), ((0, 0), (1, 1), (0, 0)))
    conv = jnp.zeros((rows, cols, local_ch), jnp.float32)
    for row_off in range(3):
        for col_off in range(3):
            conv = (
                conv
                + padded[row_off : row_off + rows, col_off : col_off + cols]
                * conv_weight[row_off, col_off]
            )
    mixed = (grid_tokens.astype(jnp.float32) + conv).astype(jnp.bfloat16)
    full = lax.all_gather(mixed, "ch", axis=2, tiled=True)
    flat = full.astype(jnp.float32).reshape(count, D)
    mean = jnp.mean(flat, axis=1, keepdims=True)
    var = jnp.mean((flat - mean) ** 2, axis=1, keepdims=True)
    normed = ((flat - mean) * lax.rsqrt(var + 1e-06) * norm_gain).astype(jnp.bfloat16)
    panel = lax.all_gather(qkv_weight, "sp", axis=0, tiled=True)
    proj = jnp.dot(normed, panel.reshape(D, 3 * local_ch), preferred_element_type=jnp.float32)
    proj = proj.astype(jnp.bfloat16)
    query_local = proj[:, :local_ch]
    key_local = proj[:, local_ch : 2 * local_ch]
    value_local = proj[:, 2 * local_ch :]
    query = query_local.reshape(count, heads_here, HEAD_DIM)
    attend = make_attend(query, heads_here)
    init = start_state(heads_here, count)
    final = attend(
        init,
        (
            lax.all_gather(key_local, "sp", axis=0, tiled=True),
            lax.all_gather(value_local, "sp", axis=0, tiled=True),
        ),
        jnp.int32(0),
    )
    result = final[2] / final[1][:, :, None]
    result = result.transpose(1, 0, 2).reshape(rows, cols, local_ch)
    return result.astype(jnp.bfloat16)


MESH = pl.DeviceIdType.MESH


def fused_kernel(
    n, x_ref, conv_ref, gain_ref, w_ref, out_ref,
    halo, mix, xs, ws, qs, ks, vs, os,
    halo_send, halo_recv, own_sem, w_send, w_recv, f_send, f_recv,
    ring_send, ring_recv, peer_send, peer_recv, out_send, out_recv,
):
    tokens, local_ch = x_ref.shape
    depth, wide = w_ref.shape[1], qs.shape[1]
    share, half = depth // 2, n // 2
    g, s, c = lax.axis_index("grp"), lax.axis_index("sp"), lax.axis_index("ch")
    pos = (s % 2) * (n - 1) + (1 - 2 * (s % 2)) * (s // 2)

    def at_ring(p):
        p = lax.rem(p + 2 * n, n)
        back = p // half
        return 2 * (p * (1 - back) + (n - 1 - p) * back) + back

    def send(src, dst, send_sem, recv_sem, to):
        return pltpu.make_async_remote_copy(
            src_ref=src, dst_ref=dst, send_sem=send_sem, recv_sem=recv_sem,
            device_id=to, device_id_type=MESH,
        )

    other_group, other_core = (1 - g, s, c), (g, s, 1 - c)

    barrier = pltpu.get_barrier_semaphore()
    for k in range(1, n):
        pl.semaphore_signal(barrier, inc=1, device_id=(g, lax.rem(s + k, n), c), device_id_type=MESH)
    pl.semaphore_signal(barrier, inc=1, device_id=other_group, device_id_type=MESH)
    pl.semaphore_signal(barrier, inc=1, device_id=other_core, device_id_type=MESH)
    pl.semaphore_wait(barrier, n + 1)

    part = local_ch // 2

    def chunk(q):
        return pl.ds(q * part, part)

    def halo_down(q):
        return send(
            x_ref.at[:, chunk(q)], halo.at[0, :, chunk(q)], halo_send.at[0, q], halo_recv.at[0, q],
            (g, lax.rem(s + 1, n), c),
        )

    def halo_up(q):
        return send(
            x_ref.at[:, chunk(q)], halo.at[1, :, chunk(q)], halo_send.at[1, q], halo_recv.at[1, q],
            (g, lax.rem(s + n - 1, n), c),
        )

    for q in range(2):

        @pl.when(s < n - 1)
        def _():
            halo_down(q).start()

        @pl.when(s > 0)
        def _():
            halo_up(q).start()

    def w_copy(k):
        to = lax.rem(s + k, n)
        cols = pl.ds(pl.multiple_of(to * wide, wide), wide)
        return send(
            w_ref.at[:, pl.ds(g * share, share), cols],
            ws.at[:, pl.ds(s * depth + g * share, share), :],
            w_send.at[k], w_recv.at[k], (g, to, c),
        )

    def w_arrived(k):
        origin = lax.rem(s + n - k, n)
        rows = ws.at[:, pl.ds(origin * depth + g * share, share), :]
        return send(rows, rows, f_send.at[k], w_recv.at[k], other_group)

    def w_forward(k):
        origin = lax.rem(s + n - k, n)
        rows = ws.at[:, pl.ds(origin * depth + g * share, share), :]
        return send(rows, rows, f_send.at[k], f_recv.at[k], other_group)

    def w_forward_in(k):
        origin = lax.rem(s + n - k, n)
        rows = ws.at[:, pl.ds(origin * depth + (1 - g) * share, share), :]
        return send(rows, rows, f_send.at[k], f_recv.at[k], other_group)

    own_w = pltpu.make_async_copy(
        w_ref.at[:, :, pl.ds(pl.multiple_of(s * wide, wide), wide)],
        ws.at[:, pl.ds(s * depth, depth), :],
        own_sem,
    )
    own_w.start()

    def start_w(k, _):
        w_copy(k).start()
        return 0

    lax.fori_loop(1, n, start_w, 0)

    @pl.when(s == 0)
    def _():
        halo[0] = jnp.zeros((tokens, local_ch), jnp.bfloat16)

    @pl.when(s == n - 1)
    def _():
        halo[1] = jnp.zeros((tokens, local_ch), jnp.bfloat16)

    def conv_part(i, _):
        cols = pl.ds(pl.multiple_of(i * 128, 128), 128)
        above = halo[0, :, cols].astype(jnp.float32)
        here = x_ref[:, cols].astype(jnp.float32)
        below = halo[1, :, cols].astype(jnp.float32)
        weight = conv_ref[:, :, cols]

        def column(b):
            return above * weight[0, b : b + 1] + here * weight[1, b : b + 1] + below * weight[2, b : b + 1]

        token = lax.broadcasted_iota(jnp.int32, (tokens, 128), 0)
        left = jnp.where(token == 0, 0.0, pltpu.roll(column(0), 1, 0))
        right = jnp.where(token == tokens - 1, 0.0, pltpu.roll(column(2), tokens - 1, 0))
        xs[s, c, :, cols] = (here + (left + column(1) + right)).astype(jnp.bfloat16)
        return 0

    def norm(owner):
        def norm_part(i, _):
            rows = pl.ds(pl.multiple_of(i * 16, 16), 16)
            first = xs[owner, 0, rows, :].astype(jnp.float32)
            second = xs[owner, 1, rows, :].astype(jnp.float32)
            channels = 2 * local_ch
            mean = (jnp.sum(first, axis=1, keepdims=True) + jnp.sum(second, axis=1, keepdims=True)) / channels
            first, second = first - mean, second - mean
            var = (
                jnp.sum(first * first, axis=1, keepdims=True) + jnp.sum(second * second, axis=1, keepdims=True)
            ) / channels
            scale = lax.rsqrt(var + 1e-06)
            mix[0, rows, :] = (first * scale * gain_ref[:, :local_ch]).astype(jnp.bfloat16)
            mix[1, rows, :] = (second * scale * gain_ref[:, local_ch:]).astype(jnp.bfloat16)
            return 0

        lax.fori_loop(0, tokens // 16, norm_part, 0)

    def pieces(way, k):
        return (0, 1) if k < half else (way,)

    def block(way, k, q, core):
        owner = at_ring(pos - k if way == 0 else pos + k)
        return xs.at[owner, core, :, chunk(q)]

    def ring_copy(way, k, q):
        piece = block(way, k - 1, q, c)
        to = (g, at_ring(pos + 1 if way == 0 else pos - 1), c)
        return send(piece, piece, ring_send.at[way, k, q], ring_recv.at[way, k, q], to)

    def ring_arrived(way, k, q):
        piece = block(way, k, q, c)
        return send(piece, piece, ring_send.at[way, k, q], ring_recv.at[way, k, q], other_core)

    def peer_copy(way, k, q):
        piece = block(way, k, q, c)
        return send(piece, piece, peer_send.at[way, k, q], peer_recv.at[way, k, q], other_core)

    def peer_arrived(way, k, q):
        piece = block(way, k, q, 1 - c)
        return send(piece, piece, peer_send.at[way, k, q], peer_recv.at[way, k, q], other_core)

    for q in range(2):

        @pl.when(s > 0)
        def _():
            halo_down(q).wait_recv()

        @pl.when(s < n - 1)
        def _():
            halo_up(q).wait_recv()

        lax.fori_loop(q * (part // 128), (q + 1) * (part // 128), conv_part, 0)
        for way in range(2):
            ring_copy(way, 1, q).start()
        peer_copy(0, 0, q).start()

    def project(owner):
        norm(owner)
        total = []
        for lo, hi in ((0, 1), (1, 3)):
            value = jnp.zeros((tokens, (hi - lo) * wide), jnp.float32)
            for h in range(2):
                weight = jnp.concatenate([ws[j, h * local_ch : (h + 1) * local_ch] for j in range(lo, hi)], axis=1)
                value = value + jnp.dot(mix[h], weight, preferred_element_type=jnp.float32)
            total.append(value)
        rows = pl.ds(pl.multiple_of(owner * tokens, tokens), tokens)
        qs[rows, :] = total[0].astype(jnp.bfloat16)
        ks[rows, :] = total[1][:, :wide].astype(jnp.bfloat16)
        vs[rows, :] = total[1][:, wide:].astype(jnp.bfloat16)

    def project_pair(k):
        def one(i, _):
            project(at_ring(pos - k + 2 * k * i))
            return 0

        lax.fori_loop(0, 2, one, 0)

    def forward_w(k, _):
        w_arrived(k).wait_recv()
        w_forward(k).start()
        return 0

    lax.fori_loop(1, n, forward_w, 0)

    for k in range(1, half + 1):
        for q in range(2):
            for way in range(2):
                if q in pieces(way, k):
                    ring_arrived(way, k, q).wait_recv()
                    if k < half and q in pieces(way, k + 1):
                        ring_copy(way, k + 1, q).start()
                    peer_copy(way, k, q).start()
        if k == 1:
            own_w.wait()

            def w_last(j, _):
                w_forward_in(j).wait_recv()
                return 0

            lax.fori_loop(1, n, w_last, 0)
            for q in range(2):
                peer_arrived(0, 0, q).wait_recv()
            project(s)
        else:
            for way in range(2):
                for q in range(2):
                    peer_arrived(way, k - 1, q).wait_recv()
            project_pair(k - 1)
    for way in range(2):
        peer_arrived(way, half, way).wait_recv()
    project(at_ring(pos + half))

    def out_copy(i):
        to = lax.rem(s + 1 + i, n)
        return send(
            os.at[i], out_ref.at[:, pl.ds(pl.multiple_of(s * wide, wide), wide)],
            out_send.at[i], out_recv.at[i], (g, to, c),
        )

    def out_arrived(i):
        origin = lax.rem(s + 2 * n - 1 - i, n)
        return send(
            os.at[i], out_ref.at[:, pl.ds(pl.multiple_of(origin * wide, wide), wide)],
            out_send.at[i], out_recv.at[i], other_core,
        )

    heads = wide // HEAD_DIM

    def attend_block(i, _):
        target = lax.rem(s + 1 + i, n)
        query = qs[pl.ds(pl.multiple_of(target * tokens, tokens), tokens), :]
        lane = lax.broadcasted_iota(jnp.int32, (tokens, wide), 1) // HEAD_DIM
        result = jnp.zeros((tokens, wide), jnp.float32)
        for h in range(heads):
            own = jnp.where(lane == h, query.astype(jnp.float32) * HEAD_DIM**-0.5, 0.0).astype(jnp.bfloat16)
            scores = lax.dot_general(
                own, ks[...], (((1,), (1,)), ((), ())), preferred_element_type=jnp.float32
            )
            top = jnp.max(scores, axis=1, keepdims=True)
            expo = jnp.exp(scores - top)
            total = jnp.sum(expo, axis=1, keepdims=True)
            part = jnp.dot(expo.astype(jnp.bfloat16), vs[...], preferred_element_type=jnp.float32)
            result = jnp.where(lane == h, part / total, result)
        os[i] = result.astype(jnp.bfloat16)

        @pl.when(i < n - 1)
        def _():
            out_copy(i).start()

        return 0

    lax.fori_loop(0, n, attend_block, 0)
    out_ref[:, pl.ds(pl.multiple_of(s * wide, wide), wide)] = os[n - 1]

    for q in range(2):

        @pl.when(s < n - 1)
        def _():
            halo_down(q).wait_send()

        @pl.when(s > 0)
        def _():
            halo_up(q).wait_send()

    def sent_w(k, _):
        w_copy(k).wait_send()
        w_forward(k).wait_send()
        return 0

    lax.fori_loop(1, n, sent_w, 0)
    for q in range(2):
        peer_copy(0, 0, q).wait_send()
    for k in range(1, half + 1):
        for way in range(2):
            for q in pieces(way, k):
                ring_copy(way, k, q).wait_send()
                peer_copy(way, k, q).wait_send()

    def out_done(i, _):
        out_copy(i).wait_send()
        out_arrived(i).wait_recv()
        return 0

    lax.fori_loop(0, n - 1, out_done, 0)


def local_fused(n, grid_tokens, conv_weight, norm_gain, qkv_weight):
    rows, cols, local_ch = grid_tokens.shape
    depth = qkv_weight.shape[0]
    wide = local_ch // n
    count = n * cols
    dma = pltpu.SemaphoreType.DMA
    vmem = pl.BlockSpec(memory_space=pltpu.VMEM)
    half = n // 2
    out = pl.pallas_call(
        functools.partial(fused_kernel, n),
        out_shape=jax.ShapeDtypeStruct((cols, local_ch), jnp.bfloat16),
        in_specs=[vmem, vmem, vmem, pl.BlockSpec(memory_space=pl.ANY)],
        out_specs=vmem,
        scratch_shapes=[
            pltpu.VMEM((2, cols, local_ch), jnp.bfloat16),
            pltpu.VMEM((2, cols, local_ch), jnp.bfloat16),
            pltpu.VMEM((n, 2, cols, local_ch), jnp.bfloat16),
            pltpu.VMEM((3, n * depth, wide), jnp.bfloat16),
            pltpu.VMEM((count, wide), jnp.bfloat16),
            pltpu.VMEM((count, wide), jnp.bfloat16),
            pltpu.VMEM((count, wide), jnp.bfloat16),
            pltpu.VMEM((n, cols, wide), jnp.bfloat16),
            dma((2, 2)), dma((2, 2)), dma, dma((n,)), dma((n,)), dma((n,)), dma((n,)),
            dma((2, half + 1, 2)), dma((2, half + 1, 2)), dma((2, half + 1, 2)), dma((2, half + 1, 2)),
            dma((n,)), dma((n,)),
        ],
        compiler_params=pltpu.CompilerParams(
            collective_id=0, has_side_effects=True, vmem_limit_bytes=40 * 1024 * 1024
        ),
    )(
        grid_tokens.reshape(cols, local_ch), conv_weight, norm_gain.reshape(1, D),
        qkv_weight.transpose(1, 0, 2),
    )
    return out.reshape(rows, cols, local_ch)


def solution(mesh):
    placed = (P(("grp", "sp"), None, "ch"), P(None, None, "ch"), P(), P("sp", None, "ch"))
    groups, n, cores = mesh.shape["grp"], mesh.shape["sp"], mesh.shape["ch"]

    def local(grid_tokens, conv_weight, norm_gain, qkv_weight):
        rows, _, local_ch = grid_tokens.shape
        if groups == 2 and cores == 2 and n % 4 == 0 and rows == 1 and local_ch == 128 * n:
            return local_fused(n, grid_tokens, conv_weight, norm_gain, qkv_weight)
        return local_gathered(grid_tokens, conv_weight, norm_gain, qkv_weight)

    return jax.shard_map(
        local, mesh=mesh, in_specs=placed, out_specs=P(("grp", "sp"), None, "ch"), check_vma=False
    )
```

```python
import functools

import jax
import jax.numpy as jnp
from jax import lax
from jax.experimental import pallas as pl
from jax.experimental.pallas import tpu as pltpu
from jax.sharding import PartitionSpec as P

D = 2048
HEAD_DIM = 64


def with_halo(block, sides, width):
    for axis, dim in sides:
        count = lax.axis_size(axis)
        forward = [(i, i + 1) for i in range(count - 1)]
        backward = [(target, source) for source, target in forward]
        low = lax.ppermute(
            lax.slice_in_dim(block, block.shape[dim] - width, None, axis=dim), axis, forward
        )
        high = lax.ppermute(lax.slice_in_dim(block, 0, width, axis=dim), axis, backward)
        block = jnp.concatenate([low, block, high], axis=dim)
    return block


def make_attend(query, heads_n):
    inv_scale = 1.0 / jnp.sqrt(jnp.float32(HEAD_DIM))

    def attend(carry, pieces, start):
        running_top, running_total, accum = carry
        key_piece, value_piece = pieces
        width = key_piece.shape[0]
        key_heads = key_piece.reshape(width, heads_n, HEAD_DIM)
        value_heads = value_piece.reshape(width, heads_n, HEAD_DIM)
        scores = (
            jnp.einsum("thd,nhd->htn", query, key_heads, preferred_element_type=jnp.float32)
            * inv_scale
        )
        new_top = jnp.maximum(running_top, jnp.max(scores, axis=2))
        expo = jnp.exp(scores - new_top[:, :, None])
        new_total = jnp.sum(expo, axis=2)
        probs = expo.astype(jnp.bfloat16)
        update = jnp.einsum("htn,nhd->htd", probs, value_heads, preferred_element_type=jnp.float32)
        return (new_top, new_total, update)

    return attend


def start_state(heads_n, queries_n):
    return (
        jnp.full((heads_n, queries_n), -1e30, jnp.float32),
        jnp.zeros((heads_n, queries_n), jnp.float32),
        jnp.zeros((heads_n, queries_n, HEAD_DIM), jnp.float32),
    )


def local_gathered(grid_tokens, conv_weight, norm_gain, qkv_weight):
    rows, cols, local_ch = grid_tokens.shape
    count = rows * cols
    heads_here = local_ch // HEAD_DIM
    extended = with_halo(grid_tokens, (("sp", 0),), 1)
    padded = jnp.pad(extended.astype(jnp.float32), ((0, 0), (1, 1), (0, 0)))
    conv = jnp.zeros((rows, cols, local_ch), jnp.float32)
    for row_off in range(3):
        for col_off in range(3):
            conv = (
                conv
                + padded[row_off : row_off + rows, col_off : col_off + cols]
                * conv_weight[row_off, col_off]
            )
    mixed = (grid_tokens.astype(jnp.float32) + conv).astype(jnp.bfloat16)
    full = lax.all_gather(mixed, "ch", axis=2, tiled=True)
    flat = full.astype(jnp.float32).reshape(count, D)
    mean = jnp.mean(flat, axis=1, keepdims=True)
    var = jnp.mean((flat - mean) ** 2, axis=1, keepdims=True)
    normed = ((flat - mean) * lax.rsqrt(var + 1e-06) * norm_gain).astype(jnp.bfloat16)
    panel = lax.all_gather(qkv_weight, "sp", axis=0, tiled=True)
    proj = jnp.dot(normed, panel.reshape(D, 3 * local_ch), preferred_element_type=jnp.float32)
    proj = proj.astype(jnp.bfloat16)
    query_local = proj[:, :local_ch]
    key_local = proj[:, local_ch : 2 * local_ch]
    value_local = proj[:, 2 * local_ch :]
    query = query_local.reshape(count, heads_here, HEAD_DIM)
    attend = make_attend(query, heads_here)
    init = start_state(heads_here, count)
    final = attend(
        init,
        (
            lax.all_gather(key_local, "sp", axis=0, tiled=True),
            lax.all_gather(value_local, "sp", axis=0, tiled=True),
        ),
        jnp.int32(0),
    )
    result = final[2] / final[1][:, :, None]
    result = result.transpose(1, 0, 2).reshape(rows, cols, local_ch)
    return result.astype(jnp.bfloat16)


MESH = pl.DeviceIdType.MESH


def fused_kernel(
    n, x_ref, conv_in, gain_in, w_ref, out_ref,
    conv_ref, gain_ref, in_sem, raw, stats, xs, ws, qs, ks, vs, os,
    own_sem, w_send, w_recv, f_send, f_recv, stat_send, stat_recv,
    ring_send, ring_recv, peer_send, peer_recv, out_send, out_recv,
):
    tokens, local_ch = x_ref.shape
    depth, wide = w_ref.shape[1], qs.shape[1]
    share, half = depth // 2, n // 2
    g, s, c = lax.axis_index("grp"), lax.axis_index("sp"), lax.axis_index("ch")
    pos = (s % 2) * (n - 1) + (1 - 2 * (s % 2)) * (s // 2)

    def at_ring(p):
        p = lax.rem(p + 2 * n, n)
        back = p // half
        return 2 * (p * (1 - back) + (n - 1 - p) * back) + back

    def send(src, dst, send_sem, recv_sem, to):
        return pltpu.make_async_remote_copy(
            src_ref=src, dst_ref=dst, send_sem=send_sem, recv_sem=recv_sem,
            device_id=to, device_id_type=MESH,
        )

    other_group, other_core = (1 - g, s, c), (g, s, 1 - c)

    own_x = pltpu.make_async_copy(x_ref, raw.at[s + 1], in_sem.at[0])
    own_conv = pltpu.make_async_copy(conv_in, conv_ref, in_sem.at[1])
    own_gain = pltpu.make_async_copy(gain_in, gain_ref, in_sem.at[2])
    own_x.start()
    own_conv.start()
    own_gain.start()
    raw[0] = jnp.zeros((tokens, local_ch), jnp.bfloat16)
    raw[n + 1] = jnp.zeros((tokens, local_ch), jnp.bfloat16)

    barrier = pltpu.get_barrier_semaphore()
    for k in range(1, n):
        pl.semaphore_signal(barrier, inc=1, device_id=(g, lax.rem(s + k, n), c), device_id_type=MESH)
    pl.semaphore_signal(barrier, inc=1, device_id=other_group, device_id_type=MESH)
    pl.semaphore_signal(barrier, inc=1, device_id=other_core, device_id_type=MESH)
    pl.semaphore_wait(barrier, n + 1)

    def w_copy(k):
        to = lax.rem(s + k, n)
        cols = pl.ds(pl.multiple_of(to * wide, wide), wide)
        return send(
            w_ref.at[:, pl.ds(g * share, share), cols],
            ws.at[:, pl.ds(s * depth + g * share, share), :],
            w_send.at[k], w_recv.at[k], (g, to, c),
        )

    def w_arrived(k):
        origin = lax.rem(s + n - k, n)
        rows = ws.at[:, pl.ds(origin * depth + g * share, share), :]
        return send(rows, rows, f_send.at[k], w_recv.at[k], other_group)

    def w_forward(k):
        origin = lax.rem(s + n - k, n)
        rows = ws.at[:, pl.ds(origin * depth + g * share, share), :]
        return send(rows, rows, f_send.at[k], f_recv.at[k], other_group)

    def w_forward_in(k):
        origin = lax.rem(s + n - k, n)
        rows = ws.at[:, pl.ds(origin * depth + (1 - g) * share, share), :]
        return send(rows, rows, f_send.at[k], f_recv.at[k], other_group)

    own_w = pltpu.make_async_copy(
        w_ref.at[:, :, pl.ds(pl.multiple_of(s * wide, wide), wide)],
        ws.at[:, pl.ds(s * depth, depth), :],
        own_sem,
    )
    own_w.start()

    def start_w(k, _):
        w_copy(k).start()
        return 0


    def mix_row(r):
        def conv_part(i, _):
            cols = pl.ds(pl.multiple_of(i * 128, 128), 128)
            above = raw[r, :, cols].astype(jnp.float32)
            here = raw[r + 1, :, cols].astype(jnp.float32)
            below = raw[r + 2, :, cols].astype(jnp.float32)
            weight = conv_ref[:, :, cols]

            def column(b):
                return above * weight[0, b : b + 1] + here * weight[1, b : b + 1] + below * weight[2, b : b + 1]

            token = lax.broadcasted_iota(jnp.int32, (tokens, 128), 0)
            left = jnp.where(token == 0, 0.0, pltpu.roll(column(0), 1, 0))
            right = jnp.where(token == tokens - 1, 0.0, pltpu.roll(column(2), tokens - 1, 0))
            xs[r, c, :, cols] = (here + (left + column(1) + right)).astype(jnp.bfloat16)
            return 0

        lax.fori_loop(0, local_ch // 128, conv_part, 0)

        def stat_part(i, _):
            rows = pl.ds(pl.multiple_of(i * 32, 32), 32)
            values = xs[r, c, rows, :].astype(jnp.float32)
            mean = jnp.sum(values, axis=1, keepdims=True) / local_ch
            values = values - mean
            spread = jnp.sum(values * values, axis=1, keepdims=True)
            stats[r, c, 0, rows, :] = jnp.broadcast_to(mean, (32, 128))
            stats[r, c, 1, rows, :] = jnp.broadcast_to(spread, (32, 128))
            return 0

        lax.fori_loop(0, tokens // 32, stat_part, 0)
        stat_copy(r, c).start()

    def stat_copy(r, core):
        return send(stats.at[r, core], stats.at[r, core], stat_send.at[r], stat_recv.at[r], other_core)

    def row_copy(r, core):
        return send(xs.at[r, core], xs.at[r, core], peer_send.at[r], peer_recv.at[r], other_core)

    def norm_row(r):
        stat_copy(r, 1 - c).wait_recv()
        gain = gain_ref[:, pl.ds(pl.multiple_of(c * local_ch, local_ch), local_ch)]

        def norm_part(i, _):
            rows = pl.ds(pl.multiple_of(i * 32, 32), 32)
            mean_0, mean_1 = stats[r, 0, 0, rows, :1], stats[r, 1, 0, rows, :1]
            gap = mean_0 - mean_1
            mean = 0.5 * (mean_0 + mean_1)
            spread = stats[r, 0, 1, rows, :1] + stats[r, 1, 1, rows, :1] + gap * gap * (0.5 * local_ch)
            scale = lax.rsqrt(spread / (2 * local_ch) + 1e-06)
            values = xs[r, c, rows, :].astype(jnp.float32)
            xs[r, c, rows, :] = ((values - mean) * scale * gain).astype(jnp.bfloat16)
            return 0

        lax.fori_loop(0, tokens // 32, norm_part, 0)
        row_copy(r, c).start()

    def ring_block(way, k, split):
        owner = at_ring(pos - k if way == 0 else pos + k)
        if not split:
            return raw.at[owner + 1]
        return raw.at[owner + 1, pl.ds(way * (tokens // 2), tokens // 2)]

    def ring_copy(way, k):
        part = ring_block(way, k - 1, k == half)
        to = (g, at_ring(pos + 1 if way == 0 else pos - 1), c)
        return send(part, part, ring_send.at[way, k], ring_recv.at[way, k], to)

    def ring_arrived(way, k):
        part = ring_block(way, k, k == half)
        return send(part, part, ring_send.at[way, k], ring_recv.at[way, k], other_core)

    def steps(r):
        away = lax.rem((r % 2) * (n - 1) + (1 - 2 * (r % 2)) * (r // 2) - pos + n, n)
        return away + (n - 2 * away) * (away // (half + 1))

    def ready(r):
        return jnp.maximum(steps(r), jnp.maximum(steps(jnp.maximum(r - 1, 0)), steps(jnp.minimum(r + 1, n - 1))))

    def for_rows(k, act):
        def one(r, _):
            @pl.when(ready(r) == k)
            def _():
                act(r)

            return 0

        lax.fori_loop(0, n, one, 0)

    def project(owner):
        total = []
        for lo, hi in ((0, 1), (1, 3)):
            value = jnp.zeros((tokens, (hi - lo) * wide), jnp.float32)
            for h in range(2):
                weight = jnp.concatenate([ws[j, h * local_ch : (h + 1) * local_ch] for j in range(lo, hi)], axis=1)
                value = value + jnp.dot(xs[owner, h], weight, preferred_element_type=jnp.float32)
            total.append(value)
        rows = pl.ds(pl.multiple_of(owner * tokens, tokens), tokens)
        qs[rows, :] = total[0].astype(jnp.bfloat16)
        ks[rows, :] = total[1][:, :wide].astype(jnp.bfloat16)
        vs[rows, :] = total[1][:, wide:].astype(jnp.bfloat16)

    def finish_row(r):
        row_copy(r, 1 - c).wait_recv()
        project(r)

    def forward_w(k, _):
        w_arrived(k).wait_recv()
        w_forward(k).start()
        return 0


    own_x.wait()
    for way in range(2):
        ring_copy(way, 1).start()
    lax.fori_loop(1, n, start_w, 0)
    own_conv.wait()
    own_gain.wait()

    for k in range(1, half + 1):
        for way in range(2):
            ring_arrived(way, k).wait_recv()
            if k < half:
                ring_copy(way, k + 1).start()
        for_rows(k, mix_row)
        if k < 3:
            lax.fori_loop(1 + (k - 1) * (n - 1) // 2, 1 + k * (n - 1) // 2, forward_w, 0)
        for_rows(k, norm_row)
        if k == half:
            own_w.wait()

            def w_last(j, _):
                w_forward_in(j).wait_recv()
                return 0

            lax.fori_loop(1, n, w_last, 0)
            for j in range(1, half):
                for_rows(j, finish_row)
    for_rows(half, finish_row)

    def out_copy(i):
        to = lax.rem(s + 1 + i, n)
        return send(
            os.at[i], out_ref.at[:, pl.ds(pl.multiple_of(s * wide, wide), wide)],
            out_send.at[i], out_recv.at[i], (g, to, c),
        )

    def out_arrived(i):
        origin = lax.rem(s + 2 * n - 1 - i, n)
        return send(
            os.at[i], out_ref.at[:, pl.ds(pl.multiple_of(origin * wide, wide), wide)],
            out_send.at[i], out_recv.at[i], other_core,
        )

    heads = wide // HEAD_DIM

    def attend_block(i, _):
        block = lax.rem(s + 1 + i, n)
        query = qs[pl.ds(pl.multiple_of(block * tokens, tokens), tokens), :]
        lane = lax.broadcasted_iota(jnp.int32, (tokens, wide), 1) // HEAD_DIM
        result = jnp.zeros((tokens, wide), jnp.float32)
        for h in range(heads):
            own = jnp.where(lane == h, query.astype(jnp.float32) * HEAD_DIM**-0.5, 0.0).astype(jnp.bfloat16)
            scores = lax.dot_general(
                own, ks[...], (((1,), (1,)), ((), ())), preferred_element_type=jnp.float32
            )
            top = jnp.max(scores, axis=1, keepdims=True)
            expo = jnp.exp(scores - top)
            total = jnp.sum(expo, axis=1, keepdims=True)
            part = jnp.dot(expo.astype(jnp.bfloat16), vs[...], preferred_element_type=jnp.float32)
            result = jnp.where(lane == h, part / total, result)
        os[i] = result.astype(jnp.bfloat16)

        @pl.when(i < n - 1)
        def _():
            out_copy(i).start()

        return 0

    lax.fori_loop(0, n, attend_block, 0)
    out_ref[:, pl.ds(pl.multiple_of(s * wide, wide), wide)] = os[n - 1]

    def sent_w(k, _):
        w_copy(k).wait_send()
        w_forward(k).wait_send()
        return 0

    lax.fori_loop(1, n, sent_w, 0)
    for k in range(1, half + 1):
        for way in range(2):
            ring_copy(way, k).wait_send()

    def sent_row(r, _):
        stat_copy(r, c).wait_send()
        row_copy(r, c).wait_send()
        return 0

    lax.fori_loop(0, n, sent_row, 0)

    def out_done(i, _):
        out_copy(i).wait_send()
        out_arrived(i).wait_recv()
        return 0

    lax.fori_loop(0, n - 1, out_done, 0)


def local_fused(n, grid_tokens, conv_weight, norm_gain, qkv_weight):
    rows, cols, local_ch = grid_tokens.shape
    depth = qkv_weight.shape[0]
    wide = local_ch // n
    count = n * cols
    dma = pltpu.SemaphoreType.DMA
    vmem = pl.BlockSpec(memory_space=pltpu.VMEM)
    half = n // 2
    out = pl.pallas_call(
        functools.partial(fused_kernel, n),
        out_shape=jax.ShapeDtypeStruct((cols, local_ch), jnp.bfloat16),
        in_specs=[pl.BlockSpec(memory_space=pltpu.HBM)] * 4,
        out_specs=vmem,
        scratch_shapes=[
            pltpu.VMEM(conv_weight.shape, jnp.float32),
            pltpu.VMEM((1, D), jnp.float32),
            dma((3,)),
            pltpu.VMEM((n + 2, cols, local_ch), jnp.bfloat16),
            pltpu.VMEM((n, 2, 2, cols, 128), jnp.float32),
            pltpu.VMEM((n, 2, cols, local_ch), jnp.bfloat16),
            pltpu.VMEM((3, n * depth, wide), jnp.bfloat16),
            pltpu.VMEM((count, wide), jnp.bfloat16),
            pltpu.VMEM((count, wide), jnp.bfloat16),
            pltpu.VMEM((count, wide), jnp.bfloat16),
            pltpu.VMEM((n, cols, wide), jnp.bfloat16),
            dma, dma((n,)), dma((n,)), dma((n,)), dma((n,)), dma((n,)), dma((n,)),
            dma((2, half + 1)), dma((2, half + 1)), dma((n,)), dma((n,)),
            dma((n,)), dma((n,)),
        ],
        compiler_params=pltpu.CompilerParams(
            collective_id=0, has_side_effects=True, vmem_limit_bytes=63 * 1024 * 1024
        ),
    )(
        grid_tokens.reshape(cols, local_ch), conv_weight, norm_gain.reshape(1, D),
        qkv_weight.transpose(1, 0, 2),
    )
    return out.reshape(rows, cols, local_ch)


def solution(mesh):
    placed = (P(("grp", "sp"), None, "ch"), P(None, None, "ch"), P(), P("sp", None, "ch"))
    groups, n, cores = mesh.shape["grp"], mesh.shape["sp"], mesh.shape["ch"]

    def local(grid_tokens, conv_weight, norm_gain, qkv_weight):
        rows, _, local_ch = grid_tokens.shape
        if groups == 2 and cores == 2 and n % 4 == 0 and rows == 1 and local_ch == 128 * n:
            return local_fused(n, grid_tokens, conv_weight, norm_gain, qkv_weight)
        return local_gathered(grid_tokens, conv_weight, norm_gain, qkv_weight)

    return jax.shard_map(
        local, mesh=mesh, in_specs=placed, out_specs=P(("grp", "sp"), None, "ch"), check_vma=False
    )
```

```python
import functools

import jax
import jax.numpy as jnp
from jax import lax
from jax.experimental import pallas as pl
from jax.experimental.pallas import tpu as pltpu
from jax.sharding import PartitionSpec as P

D = 2048
HEAD_DIM = 64


def with_halo(block, sides, width):
    for axis, dim in sides:
        count = lax.axis_size(axis)
        forward = [(i, i + 1) for i in range(count - 1)]
        backward = [(target, source) for source, target in forward]
        low = lax.ppermute(
            lax.slice_in_dim(block, block.shape[dim] - width, None, axis=dim), axis, forward
        )
        high = lax.ppermute(lax.slice_in_dim(block, 0, width, axis=dim), axis, backward)
        block = jnp.concatenate([low, block, high], axis=dim)
    return block


def make_attend(query, heads_n):
    inv_scale = 1.0 / jnp.sqrt(jnp.float32(HEAD_DIM))

    def attend(carry, pieces, start):
        running_top, running_total, accum = carry
        key_piece, value_piece = pieces
        width = key_piece.shape[0]
        key_heads = key_piece.reshape(width, heads_n, HEAD_DIM)
        value_heads = value_piece.reshape(width, heads_n, HEAD_DIM)
        scores = (
            jnp.einsum("thd,nhd->htn", query, key_heads, preferred_element_type=jnp.float32)
            * inv_scale
        )
        new_top = jnp.maximum(running_top, jnp.max(scores, axis=2))
        expo = jnp.exp(scores - new_top[:, :, None])
        new_total = jnp.sum(expo, axis=2)
        probs = expo.astype(jnp.bfloat16)
        update = jnp.einsum("htn,nhd->htd", probs, value_heads, preferred_element_type=jnp.float32)
        return (new_top, new_total, update)

    return attend


def start_state(heads_n, queries_n):
    return (
        jnp.full((heads_n, queries_n), -1e30, jnp.float32),
        jnp.zeros((heads_n, queries_n), jnp.float32),
        jnp.zeros((heads_n, queries_n, HEAD_DIM), jnp.float32),
    )


def local_gathered(grid_tokens, conv_weight, norm_gain, qkv_weight):
    rows, cols, local_ch = grid_tokens.shape
    count = rows * cols
    heads_here = local_ch // HEAD_DIM
    extended = with_halo(grid_tokens, (("sp", 0),), 1)
    padded = jnp.pad(extended.astype(jnp.float32), ((0, 0), (1, 1), (0, 0)))
    conv = jnp.zeros((rows, cols, local_ch), jnp.float32)
    for row_off in range(3):
        for col_off in range(3):
            conv = (
                conv
                + padded[row_off : row_off + rows, col_off : col_off + cols]
                * conv_weight[row_off, col_off]
            )
    mixed = (grid_tokens.astype(jnp.float32) + conv).astype(jnp.bfloat16)
    full = lax.all_gather(mixed, "ch", axis=2, tiled=True)
    flat = full.astype(jnp.float32).reshape(count, D)
    mean = jnp.mean(flat, axis=1, keepdims=True)
    var = jnp.mean((flat - mean) ** 2, axis=1, keepdims=True)
    normed = ((flat - mean) * lax.rsqrt(var + 1e-06) * norm_gain).astype(jnp.bfloat16)
    panel = lax.all_gather(qkv_weight, "sp", axis=0, tiled=True)
    proj = jnp.dot(normed, panel.reshape(D, 3 * local_ch), preferred_element_type=jnp.float32)
    proj = proj.astype(jnp.bfloat16)
    query_local = proj[:, :local_ch]
    key_local = proj[:, local_ch : 2 * local_ch]
    value_local = proj[:, 2 * local_ch :]
    query = query_local.reshape(count, heads_here, HEAD_DIM)
    attend = make_attend(query, heads_here)
    init = start_state(heads_here, count)
    final = attend(
        init,
        (
            lax.all_gather(key_local, "sp", axis=0, tiled=True),
            lax.all_gather(value_local, "sp", axis=0, tiled=True),
        ),
        jnp.int32(0),
    )
    result = final[2] / final[1][:, :, None]
    result = result.transpose(1, 0, 2).reshape(rows, cols, local_ch)
    return result.astype(jnp.bfloat16)


MESH = pl.DeviceIdType.MESH


def fused_kernel(
    n, x_ref, conv_in, gain_in, w_ref, out_ref,
    conv_ref, gain_ref, in_sem, raw, stats, xs, ws, qs, ks, vs, os,
    own_sem, w_send, w_recv, f_send, f_recv, stat_send, stat_recv,
    ring_send, ring_recv, peer_send, peer_recv, out_send, out_recv,
):
    tokens, local_ch = x_ref.shape
    depth, wide = w_ref.shape[1], qs.shape[1]
    share, half = depth // 2, n // 2
    g, s, c = lax.axis_index("grp"), lax.axis_index("sp"), lax.axis_index("ch")
    pos = (s % 2) * (n - 1) + (1 - 2 * (s % 2)) * (s // 2)

    def at_ring(p):
        p = lax.rem(p + 2 * n, n)
        back = p // half
        return 2 * (p * (1 - back) + (n - 1 - p) * back) + back

    def send(src, dst, send_sem, recv_sem, to):
        return pltpu.make_async_remote_copy(
            src_ref=src, dst_ref=dst, send_sem=send_sem, recv_sem=recv_sem,
            device_id=to, device_id_type=MESH,
        )

    other_group, other_core = (1 - g, s, c), (g, s, 1 - c)

    own_x = pltpu.make_async_copy(x_ref, raw.at[s + 1], in_sem.at[0])
    own_conv = pltpu.make_async_copy(conv_in, conv_ref, in_sem.at[1])
    own_gain = pltpu.make_async_copy(gain_in, gain_ref, in_sem.at[2])
    own_x.start()
    own_conv.start()
    own_gain.start()
    raw[0] = jnp.zeros((tokens, local_ch), jnp.bfloat16)
    raw[n + 1] = jnp.zeros((tokens, local_ch), jnp.bfloat16)

    barrier = pltpu.get_barrier_semaphore()
    for k in range(1, n):
        pl.semaphore_signal(barrier, inc=1, device_id=(g, lax.rem(s + k, n), c), device_id_type=MESH)
    pl.semaphore_signal(barrier, inc=1, device_id=other_group, device_id_type=MESH)
    pl.semaphore_signal(barrier, inc=1, device_id=other_core, device_id_type=MESH)
    pl.semaphore_wait(barrier, n + 1)

    def w_copy(k):
        to = lax.rem(s + k, n)
        cols = pl.ds(pl.multiple_of(to * wide, wide), wide)
        return send(
            w_ref.at[:, pl.ds(g * share, share), cols],
            ws.at[:, pl.ds(s * depth + g * share, share), :],
            w_send.at[k], w_recv.at[k], (g, to, c),
        )

    def w_arrived(k):
        origin = lax.rem(s + n - k, n)
        rows = ws.at[:, pl.ds(origin * depth + g * share, share), :]
        return send(rows, rows, f_send.at[k], w_recv.at[k], other_group)

    def w_forward(k):
        origin = lax.rem(s + n - k, n)
        rows = ws.at[:, pl.ds(origin * depth + g * share, share), :]
        return send(rows, rows, f_send.at[k], f_recv.at[k], other_group)

    def w_forward_in(k):
        origin = lax.rem(s + n - k, n)
        rows = ws.at[:, pl.ds(origin * depth + (1 - g) * share, share), :]
        return send(rows, rows, f_send.at[k], f_recv.at[k], other_group)

    own_w = pltpu.make_async_copy(
        w_ref.at[:, :, pl.ds(pl.multiple_of(s * wide, wide), wide)],
        ws.at[:, pl.ds(s * depth, depth), :],
        own_sem,
    )
    own_w.start()

    def start_w(k, _):
        w_copy(k).start()
        return 0


    def mix_row(r):
        def conv_part(i, _):
            cols = pl.ds(pl.multiple_of(i * 128, 128), 128)
            above = raw[r, :, cols].astype(jnp.float32)
            here = raw[r + 1, :, cols].astype(jnp.float32)
            below = raw[r + 2, :, cols].astype(jnp.float32)
            weight = conv_ref[:, :, cols]

            def column(b):
                return above * weight[0, b : b + 1] + here * weight[1, b : b + 1] + below * weight[2, b : b + 1]

            token = lax.broadcasted_iota(jnp.int32, (tokens, 128), 0)
            left = jnp.where(token == 0, 0.0, pltpu.roll(column(0), 1, 0))
            right = jnp.where(token == tokens - 1, 0.0, pltpu.roll(column(2), tokens - 1, 0))
            xs[r, c, :, cols] = (here + (left + column(1) + right)).astype(jnp.bfloat16)
            return 0

        lax.fori_loop(0, local_ch // 128, conv_part, 0, unroll=2)

        def stat_part(i, _):
            rows = pl.ds(pl.multiple_of(i * 32, 32), 32)
            values = xs[r, c, rows, :].astype(jnp.float32)
            mean = jnp.sum(values, axis=1, keepdims=True) / local_ch
            values = values - mean
            spread = jnp.sum(values * values, axis=1, keepdims=True)
            stats[r, c, 0, rows, :] = jnp.broadcast_to(mean, (32, 128))
            stats[r, c, 1, rows, :] = jnp.broadcast_to(spread, (32, 128))
            return 0

        lax.fori_loop(0, tokens // 32, stat_part, 0, unroll=2)
        stat_copy(r, c).start()

    def stat_copy(r, core):
        return send(stats.at[r, core], stats.at[r, core], stat_send.at[r], stat_recv.at[r], other_core)

    def row_copy(r, core):
        return send(xs.at[r, core], xs.at[r, core], peer_send.at[r], peer_recv.at[r], other_core)

    def norm_row(r):
        stat_copy(r, 1 - c).wait_recv()
        gain = gain_ref[:, pl.ds(pl.multiple_of(c * local_ch, local_ch), local_ch)]

        def norm_part(i, _):
            rows = pl.ds(pl.multiple_of(i * 32, 32), 32)
            mean_0, mean_1 = stats[r, 0, 0, rows, :1], stats[r, 1, 0, rows, :1]
            gap = mean_0 - mean_1
            mean = 0.5 * (mean_0 + mean_1)
            spread = stats[r, 0, 1, rows, :1] + stats[r, 1, 1, rows, :1] + gap * gap * (0.5 * local_ch)
            scale = lax.rsqrt(spread / (2 * local_ch) + 1e-06)
            values = xs[r, c, rows, :].astype(jnp.float32)
            xs[r, c, rows, :] = ((values - mean) * scale * gain).astype(jnp.bfloat16)
            return 0

        lax.fori_loop(0, tokens // 32, norm_part, 0, unroll=2)
        row_copy(r, c).start()

    def ring_block(way, k, split):
        owner = at_ring(pos - k if way == 0 else pos + k)
        if not split:
            return raw.at[owner + 1]
        return raw.at[owner + 1, pl.ds(way * (tokens // 2), tokens // 2)]

    def ring_copy(way, k):
        part = ring_block(way, k - 1, k == half)
        to = (g, at_ring(pos + 1 if way == 0 else pos - 1), c)
        return send(part, part, ring_send.at[way, k], ring_recv.at[way, k], to)

    def ring_arrived(way, k):
        part = ring_block(way, k, k == half)
        return send(part, part, ring_send.at[way, k], ring_recv.at[way, k], other_core)

    def steps(r):
        away = lax.rem((r % 2) * (n - 1) + (1 - 2 * (r % 2)) * (r // 2) - pos + n, n)
        return away + (n - 2 * away) * (away // (half + 1))

    def ready(r):
        return jnp.maximum(steps(r), jnp.maximum(steps(jnp.maximum(r - 1, 0)), steps(jnp.minimum(r + 1, n - 1))))

    def for_rows(k, act):
        def one(r, _):
            @pl.when(ready(r) == k)
            def _():
                act(r)

            return 0

        lax.fori_loop(0, n, one, 0)

    def project(owner):
        total = []
        for lo, hi in ((0, 1), (1, 3)):
            value = jnp.zeros((tokens, (hi - lo) * wide), jnp.float32)
            for h in range(2):
                weight = jnp.concatenate([ws[j, h * local_ch : (h + 1) * local_ch] for j in range(lo, hi)], axis=1)
                value = value + jnp.dot(xs[owner, h], weight, preferred_element_type=jnp.float32)
            total.append(value)
        rows = pl.ds(pl.multiple_of(owner * tokens, tokens), tokens)
        qs[rows, :] = total[0].astype(jnp.bfloat16)
        ks[rows, :] = total[1][:, :wide].astype(jnp.bfloat16)
        vs[rows, :] = total[1][:, wide:].astype(jnp.bfloat16)

    def finish_row(r):
        row_copy(r, 1 - c).wait_recv()
        project(r)

    def forward_w(k, _):
        w_arrived(k).wait_recv()
        w_forward(k).start()
        return 0


    own_x.wait()
    for way in range(2):
        ring_copy(way, 1).start()
    lax.fori_loop(1, n, start_w, 0)
    own_conv.wait()
    own_gain.wait()

    for k in range(1, half + 1):
        for way in range(2):
            ring_arrived(way, k).wait_recv()
            if k < half:
                ring_copy(way, k + 1).start()
        for_rows(k, mix_row)
        if k < 3:
            lax.fori_loop(1 + (k - 1) * (n - 1) // 2, 1 + k * (n - 1) // 2, forward_w, 0)
        for_rows(k, norm_row)
        if k == half:
            own_w.wait()

            def w_last(j, _):
                w_forward_in(j).wait_recv()
                return 0

            lax.fori_loop(1, n, w_last, 0)
            for j in range(1, half):
                for_rows(j, finish_row)
    for_rows(half, finish_row)

    def out_copy(i):
        to = lax.rem(s + 1 + i, n)
        return send(
            os.at[i], out_ref.at[:, pl.ds(pl.multiple_of(s * wide, wide), wide)],
            out_send.at[i], out_recv.at[i], (g, to, c),
        )

    def out_arrived(i):
        origin = lax.rem(s + 2 * n - 1 - i, n)
        return send(
            os.at[i], out_ref.at[:, pl.ds(pl.multiple_of(origin * wide, wide), wide)],
            out_send.at[i], out_recv.at[i], other_core,
        )

    heads = wide // HEAD_DIM

    def attend_block(i, _):
        block = lax.rem(s + 1 + i, n)
        query = qs[pl.ds(pl.multiple_of(block * tokens, tokens), tokens), :]
        lane = lax.broadcasted_iota(jnp.int32, (tokens, wide), 1) // HEAD_DIM
        result = jnp.zeros((tokens, wide), jnp.float32)
        for h in range(heads):
            own = jnp.where(lane == h, query.astype(jnp.float32) * HEAD_DIM**-0.5, 0.0).astype(jnp.bfloat16)
            scores = lax.dot_general(
                own, ks[...], (((1,), (1,)), ((), ())), preferred_element_type=jnp.float32
            )
            top = jnp.max(scores, axis=1, keepdims=True)
            expo = jnp.exp(scores - top)
            total = jnp.sum(expo, axis=1, keepdims=True)
            part = jnp.dot(expo.astype(jnp.bfloat16), vs[...], preferred_element_type=jnp.float32)
            result = jnp.where(lane == h, part / total, result)
        os[i] = result.astype(jnp.bfloat16)

        @pl.when(i < n - 1)
        def _():
            out_copy(i).start()

        return 0

    lax.fori_loop(0, n, attend_block, 0)
    out_ref[:, pl.ds(pl.multiple_of(s * wide, wide), wide)] = os[n - 1]

    def sent_w(k, _):
        w_copy(k).wait_send()
        w_forward(k).wait_send()
        return 0

    lax.fori_loop(1, n, sent_w, 0)
    for k in range(1, half + 1):
        for way in range(2):
            ring_copy(way, k).wait_send()

    def sent_row(r, _):
        stat_copy(r, c).wait_send()
        row_copy(r, c).wait_send()
        return 0

    lax.fori_loop(0, n, sent_row, 0)

    def out_done(i, _):
        out_copy(i).wait_send()
        out_arrived(i).wait_recv()
        return 0

    lax.fori_loop(0, n - 1, out_done, 0)


def local_fused(n, grid_tokens, conv_weight, norm_gain, qkv_weight):
    rows, cols, local_ch = grid_tokens.shape
    depth = qkv_weight.shape[0]
    wide = local_ch // n
    count = n * cols
    dma = pltpu.SemaphoreType.DMA
    vmem = pl.BlockSpec(memory_space=pltpu.VMEM)
    half = n // 2
    out = pl.pallas_call(
        functools.partial(fused_kernel, n),
        out_shape=jax.ShapeDtypeStruct((cols, local_ch), jnp.bfloat16),
        in_specs=[pl.BlockSpec(memory_space=pltpu.HBM)] * 4,
        out_specs=vmem,
        scratch_shapes=[
            pltpu.VMEM(conv_weight.shape, jnp.float32),
            pltpu.VMEM((1, D), jnp.float32),
            dma((3,)),
            pltpu.VMEM((n + 2, cols, local_ch), jnp.bfloat16),
            pltpu.VMEM((n, 2, 2, cols, 128), jnp.float32),
            pltpu.VMEM((n, 2, cols, local_ch), jnp.bfloat16),
            pltpu.VMEM((3, n * depth, wide), jnp.bfloat16),
            pltpu.VMEM((count, wide), jnp.bfloat16),
            pltpu.VMEM((count, wide), jnp.bfloat16),
            pltpu.VMEM((count, wide), jnp.bfloat16),
            pltpu.VMEM((n, cols, wide), jnp.bfloat16),
            dma, dma((n,)), dma((n,)), dma((n,)), dma((n,)), dma((n,)), dma((n,)),
            dma((2, half + 1)), dma((2, half + 1)), dma((n,)), dma((n,)),
            dma((n,)), dma((n,)),
        ],
        compiler_params=pltpu.CompilerParams(
            collective_id=0, has_side_effects=True, vmem_limit_bytes=63 * 1024 * 1024
        ),
    )(
        grid_tokens.reshape(cols, local_ch), conv_weight, norm_gain.reshape(1, D),
        qkv_weight.transpose(1, 0, 2),
    )
    return out.reshape(rows, cols, local_ch)


def solution(mesh):
    placed = (P(("grp", "sp"), None, "ch"), P(None, None, "ch"), P(), P("sp", None, "ch"))
    groups, n, cores = mesh.shape["grp"], mesh.shape["sp"], mesh.shape["ch"]

    def local(grid_tokens, conv_weight, norm_gain, qkv_weight):
        rows, _, local_ch = grid_tokens.shape
        if groups == 2 and cores == 2 and n % 4 == 0 and rows == 1 and local_ch == 128 * n:
            return local_fused(n, grid_tokens, conv_weight, norm_gain, qkv_weight)
        return local_gathered(grid_tokens, conv_weight, norm_gain, qkv_weight)

    return jax.shard_map(
        local, mesh=mesh, in_specs=placed, out_specs=P(("grp", "sp"), None, "ch"), check_vma=False
    )
```
